768 devices in a mesh: dp: 128 (over z_lo, x, y), tensor: 6 (over z_hi, core).
Axes of the slice: x: 4, y: 8, z: 12 (z_hi: 3, z_lo: 4; z = z_hi * 4 + z_lo), core: 2. Of those that a mesh axis runs over, the one named last changes fastest.
Arguments:
- inputs: bfloat16 [2048, 6144], P('dp', 'tensor'), may hold values from -6 to 6
- in_basis: bfloat16 [48, 128, 128], P('tensor'), may hold values from -0.5 to 0.5
- out_grads: bfloat16 [2048, 6144], P('dp', 'tensor'), may hold values from -6 to 6
- out_basis: bfloat16 [6144, 6144], P('tensor', 'dp'), may hold values from -0.078125 to 0.078125
Outputs:
- eigen_values: float32 [6144, 6144], P('tensor', 'dp')
The draws below stay inside these ranges and needn't reach their ends.
All inputs are finite; a program needn't handle non-finite values.
Results may differ from the reference program's by a relative error of at most 0.00041.
Values may be sent and summed in bfloat16 or wider, within the bound.
A program may use at most 32 MiB of HBM per device.

```python
import jax
import jax.numpy as jnp

HEADS = 48
HEAD_DIM = 128
DG = 6144
DA = 6144
TOKENS = 2048


def block_scale(rng, shape, shards, low, high):
    def one(dim, shards_of):
        draws = jax.random.uniform(jax.random.fold_in(jax.random.fold_in(rng, 6), dim), (shards_of,), jnp.float32, low / len(shards), high / len(shards))
        return jnp.repeat(jnp.exp(draws), shape[dim] // shards_of).reshape((-1,) + (1,) * (len(shape) - dim - 1))

    gain = one(*shards[0])
    for cut in shards[1:]:
        gain = gain * one(*cut)
    return gain


def centred(own_key, dims, deviation, most, pieces=(), held_as=jnp.bfloat16):
    drawn = deviation * jax.random.normal(own_key, dims, jnp.float32)
    if pieces:
        drawn = drawn * block_scale(own_key, dims, pieces, -0.22, 0.18)
    return jnp.clip(drawn, -most, most).astype(held_as)


def setup_inputs(seed: int = 0) -> dict:
    arg_keys = jax.random.split(jax.random.key(seed), 5)
    inputs = centred(arg_keys[0], (TOKENS, DA), 1.0, 6.0, ((0, 128), (1, 6)))
    in_basis = centred(arg_keys[1], (HEADS, HEAD_DIM, HEAD_DIM), HEAD_DIM ** -0.5, 0.5, ((0, 6),))
    out_grads = centred(arg_keys[2], (TOKENS, DG), 1.0, 6.0, ((0, 128), (1, 6)))
    out_basis = centred(arg_keys[3], (DG, DG), DG ** -0.5, 0.078125, ((0, 6), (1, 128)))
    return dict(inputs=inputs, in_basis=in_basis, out_grads=out_grads, out_basis=out_basis)


def reference(inputs, in_basis, out_grads, out_basis):
    token_count = inputs.shape[0]
    split_heads = inputs.reshape(token_count, HEADS, HEAD_DIM).astype(jnp.float32)
    rotated_in = jnp.einsum("thd,hde->the", split_heads, in_basis.astype(jnp.float32))
    rotated_in = rotated_in.reshape(token_count, HEADS * HEAD_DIM)
    square_in = (rotated_in * rotated_in).astype(jnp.bfloat16)
    rotated_out = jnp.dot(out_grads, out_basis, preferred_element_type=jnp.float32)
    square_out = (rotated_out * rotated_out).astype(jnp.bfloat16)
    summed = jnp.dot(square_in.T, square_out, preferred_element_type=jnp.float32)
    return summed / jnp.float32(token_count)
```

```python
import jax
import jax.numpy as jnp
from jax import lax
from jax.experimental import pallas as pl
from jax.experimental.pallas import tpu as pltpu
from jax.sharding import PartitionSpec as P

MESH = pl.DeviceIdType.MESH
BF16, F32 = jnp.bfloat16, jnp.float32
NZ, NX, NY, NH, NC = 4, 4, 8, 3, 2
NT = NH * NC
TOK, FEAT, COLS = 16, 1024, 48
HEADS, HD = 8, 128
TOKENS = 2048
SLICE = NX * COLS // NT
HALF = NY * NZ * TOK // 2
ZORDER = (0, 1, 3, 2)


def place(r):
    return (r + 2) % NY


def kernel(
    inp, basis, grad, ob, out,
    gbuf, sbuf, bbuf, inp_v, basis_v, part, part_in, sq, eig, eig_in,
    lsem, gsend, grecv, ssend, srecv, bsend, brecv, psend, precv, qsend, qrecv, esend, erecv,
):
    dp, tensor = lax.axis_index("dp"), lax.axis_index("tensor")
    zl, x, y = dp // (NX * NY), (dp // NY) % NX, dp % NY
    zh, core = tensor // NC, tensor % NC

    def at_dp(z_, x_, y_):
        return ((z_ % NZ) * NX * NY + (x_ % NX) * NY + y_ % NY, tensor)

    zpeer = {k: at_dp(zl + k, x, y) for k in range(1, NZ)}
    xpeer = {k: at_dp(zl, x + k, y) for k in range(1, NX)}
    ypeer = {1: at_dp(zl, x, y + 1), -1: at_dp(zl, x, y + NY - 1)}
    toff = [(a, b) for a in range(NH) for b in range(NC) if a or b]
    tidx = [((zh + a) % NH) * NC + (core + b) % NC for a, b in toff]
    tpeer = [(dp, t) for t in tidx]
    tback = [toff.index(((NH - a) % NH, b)) for a, b in toff]

    peers = list(zpeer.values()) + list(xpeer.values()) + list(ypeer.values()) + tpeer
    barrier = pltpu.get_barrier_semaphore()
    for p in peers:
        pl.semaphore_signal(barrier, inc=1, device_id=p, device_id_type=MESH)

    local = [
        pltpu.make_async_copy(inp, inp_v, lsem.at[0]),
        pltpu.make_async_copy(basis, basis_v, lsem.at[1]),
        pltpu.make_async_copy(grad, gbuf.at[place(0), 0], lsem.at[2]),
        pltpu.make_async_copy(ob, bbuf.at[0], lsem.at[3]),
    ]
    for c in local:
        c.start()
    pl.semaphore_wait(barrier, len(peers))

    sends = []

    def send(src, dst, ss, rs, dev):
        c = pltpu.make_async_remote_copy(
            src_ref=src, dst_ref=dst, send_sem=ss, recv_sem=rs, device_id=dev, device_id_type=MESH
        )
        c.start()
        sends.append(c)

    def landed(ref, sem):
        pltpu.make_async_copy(ref, ref, sem).wait()

    def spread(buf, ss, rs, own):
        for k in (1, 3, 2):
            zr = (NZ - k) % NZ
            send(own, buf.at[place(0), zr], ss.at[0, zr], rs.at[0, zr], zpeer[k])

    def hop(buf, ss, rs, d, own=None):
        up, down = d, (NY - d) % NY
        for i, zr in enumerate(ZORDER):
            if d == 0 and zr:
                landed(buf.at[place(0), zr], rs.at[0, zr])
            if d:
                landed(buf.at[place(up), zr], rs.at[up, zr])
            if d < 3 or i < 2:
                src = own if d == 0 and zr == 0 else buf.at[place(up), zr]
                send(src, buf.at[place(up + 1), zr], ss.at[up + 1, zr], rs.at[up + 1, zr], ypeer[1])
            if d:
                landed(buf.at[place(down), zr], rs.at[down, zr])
            if d < 3 or i >= 2:
                src = own if d == 0 and zr == 0 else buf.at[place(down), zr]
                to = (down - 1) % NY
                send(src, buf.at[place(to), zr], ss.at[to, zr], rs.at[to, zr], ypeer[-1])

    def last(buf, rs):
        for zr in ZORDER:
            landed(buf.at[place(4), zr], rs.at[4, zr])

    spread(gbuf, gsend, grecv, grad)
    for k in (1, 3, 2):
        to = NX - k
        send(ob, bbuf.at[to], bsend.at[to - 1], brecv.at[to - 1], xpeer[k])
    local[0].wait()
    local[1].wait()
    mine = sbuf.at[place(0), 0]
    for h in range(HEADS):
        cut = slice(h * HD, (h + 1) * HD)
        rot = jnp.dot(inp_v[:, cut], basis_v[h], preferred_element_type=F32)
        mine[:, cut] = (rot * rot).astype(BF16)
    hop(gbuf, gsend, grecv, 0, grad)
    spread(sbuf, ssend, srecv, mine)
    hop(gbuf, gsend, grecv, 1)
    hop(sbuf, ssend, srecv, 0, mine)
    hop(gbuf, gsend, grecv, 2)

    local[2].wait()
    local[3].wait()
    for k in range(1, NX):
        landed(bbuf.at[k], brecv.at[k - 1])

    def partial(h):
        lhs = bbuf[...].reshape(NX * COLS, FEAT)
        rhs = gbuf[4 * h : 4 * h + 4].reshape(HALF, FEAT)
        p = lax.dot_general(lhs, rhs, (((1,), (1,)), ((), ())), preferred_element_type=F32)
        part[h] = p.reshape(NT, SLICE, HALF)
        for k in range(NT - 1):
            send(
                part.at[h, tidx[k]], part_in.at[h, tback[k]],
                psend.at[h, k], precv.at[h, tback[k]], tpeer[k],
            )

    def total(h):
        acc = part[h, tensor]
        for k in range(NT - 1):
            landed(part_in.at[h, k], precv.at[h, k])
            acc = acc + part_in[h, k]
        sq[h, tensor] = (acc * acc).astype(BF16)
        for k in range(NT - 1):
            send(
                sq.at[h, tensor], sq.at[h, tensor],
                qsend.at[h, k], qrecv.at[h, tback[k]], tpeer[k],
            )

    partial(0)
    hop(sbuf, ssend, srecv, 1)
    hop(gbuf, gsend, grecv, 3)
    hop(sbuf, ssend, srecv, 2)
    last(gbuf, grecv)
    partial(1)
    total(0)
    hop(sbuf, ssend, srecv, 3)
    total(1)
    last(sbuf, srecv)
    for h in range(2):
        for k in range(NT - 1):
            landed(sq.at[h, tidx[k]], qrecv.at[h, k])
    for k in (2, 1, 3, 0):
        acc = None
        for h in range(2):
            lhs = sq[h].reshape(NX * COLS, HALF)[k * COLS : (k + 1) * COLS]
            rhs = sbuf[4 * h : 4 * h + 4].reshape(HALF, FEAT)
            p = jnp.dot(lhs, rhs, preferred_element_type=F32)
            acc = p if acc is None else acc + p
        eig[k] = acc
        if k:
            to = NX - k
            send(eig.at[k], eig_in.at[to - 1], esend.at[to - 1], erecv.at[to - 1], xpeer[k])
    acc = eig[0]
    for k in (1, 3, 2):
        landed(eig_in.at[k - 1], erecv.at[k - 1])
        acc = acc + eig_in[k - 1]
    out[...] = acc * F32(1.0 / TOKENS)
    for c in sends:
        c.wait_send()


def per_device(inputs, in_basis, out_grads, out_basis):
    dma = pltpu.SemaphoreType.DMA
    hbm = pl.BlockSpec(memory_space=pl.ANY)
    eigen = pl.pallas_call(
        kernel,
        out_shape=jax.ShapeDtypeStruct((COLS, FEAT), F32),
        in_specs=[hbm] * 4,
        out_specs=pl.BlockSpec(memory_space=pltpu.VMEM),
        scratch_shapes=[
            pltpu.VMEM((NY, NZ, TOK, FEAT), BF16),
            pltpu.VMEM((NY, NZ, TOK, FEAT), BF16),
            pltpu.VMEM((NX, COLS, FEAT), BF16),
            pltpu.VMEM((TOK, FEAT), BF16),
            pltpu.VMEM((HEADS, HD, HD), BF16),
            pltpu.VMEM((2, NT, SLICE, HALF), F32),
            pltpu.VMEM((2, NT - 1, SLICE, HALF), F32),
            pltpu.VMEM((2, NT, SLICE, HALF), BF16),
            pltpu.VMEM((NX, COLS, FEAT), F32),
            pltpu.VMEM((NX - 1, COLS, FEAT), F32),
            dma((4,)),
            dma((NY, NZ)), dma((NY, NZ)),
            dma((NY, NZ)), dma((NY, NZ)),
            dma((NX - 1,)), dma((NX - 1,)),
            dma((2, NT - 1)), dma((2, NT - 1)),
            dma((2, NT - 1)), dma((2, NT - 1)),
            dma((NX - 1,)), dma((NX - 1,)),
        ],
        compiler_params=pltpu.CompilerParams(
            collective_id=0, has_side_effects=True, vmem_limit_bytes=60 << 20
        ),
        cost_estimate=pl.CostEstimate(flops=4 * 10**8, bytes_accessed=10**6, transcendentals=0),
        name="eigen_fit",
    )(inputs, in_basis, out_grads, out_basis.T)
    return eigen.T


def solution(mesh):
    in_specs = (P("dp", "tensor"), P("tensor", None, None), P("dp", "tensor"), P("tensor", "dp"))
    out_specs = P("tensor", "dp")
    return jax.shard_map(
        per_device, mesh=mesh, in_specs=in_specs, out_specs=out_specs, check_vma=False
    )
```

```python
import jax
import jax.numpy as jnp
from jax import lax
from jax.experimental import pallas as pl
from jax.experimental.pallas import tpu as pltpu
from jax.sharding import PartitionSpec as P

MESH = pl.DeviceIdType.MESH
BF16, F32 = jnp.bfloat16, jnp.float32
NZ, NX, NY, NH, NC = 4, 4, 8, 3, 2
NT = NH * NC
NQ = 2
NP = NY // NQ
TOK, FEAT, COLS = 16, 1024, 48
FH = FEAT // 2
HEADS, HD = 8, 128
TOKENS = 2048
PTOK = NP * NZ * TOK
SLICE = NX * COLS // NT
SENDS = 128


def kernel(
    inp, basis, grad, ob, out,
    ga, gb, sbuf, bbuf, inp_v, basis_v, part, sib_in, psum, zin, away, sq, eig, eig_in,
    lsem, ssem, garecv, gbrecv, srecv, brecv, crecv, zrecv, qrecv, erecv,
):
    dp, tensor = lax.axis_index("dp"), lax.axis_index("tensor")
    zl, x, y = dp // (NX * NY), (dp // NY) % NX, dp % NY
    zh, core = tensor // NC, tensor % NC
    par, yh = y % NQ, y // NQ
    ymate = y + 1 - 2 * par

    def device(z_, x_, y_, h_=None):
        place = (z_ % NZ) * NX * NY + (x_ % NX) * NY + y_ % NY
        return (place, tensor if h_ is None else (h_ % NH) * NC + core)

    zpeer = [device(zl + k, x, y) for k in (1, 3, 2)]
    xpeer = {k: device(zl, x + k, y) for k in (2, 1, 3)}
    yfar = [device(zl, x, y + k) for k in (2, 6, 4)]
    yup, ydown = device(zl, x, y + 1), device(zl, x, y + NY - 1)
    mate = [device(zl, x, ymate, zh + a) for a in range(NH)]
    hpeer = [device(zl, x, y, zh + a) for a in (1, 2)]
    twin = (dp, zh * NC + 1 - core)

    peers = zpeer + list(xpeer.values()) + yfar + [yup, ydown] + mate[1:] + hpeer + [twin]
    barrier = pltpu.get_barrier_semaphore()
    for p in peers:
        pl.semaphore_signal(barrier, inc=1, device_id=p, device_id_type=MESH)

    lo, hi = pl.ds(0, FH), pl.ds(FH, FH)
    local = [
        pltpu.make_async_copy(inp, inp_v, lsem.at[0]),
        pltpu.make_async_copy(basis, basis_v, lsem.at[1]),
        pltpu.make_async_copy(grad.at[:, lo], ga.at[yh, zl], lsem.at[2]),
        pltpu.make_async_copy(grad.at[:, hi], gb.at[yh, zl], lsem.at[3]),
        pltpu.make_async_copy(ob, bbuf.at[par, 0], lsem.at[4]),
    ]
    for c in local:
        c.start()
    pl.semaphore_wait(barrier, len(peers))

    sends = []

    def send(src, dst, rs, dev):
        c = pltpu.make_async_remote_copy(
            src_ref=src, dst_ref=dst, send_sem=ssem.at[len(sends)], recv_sem=rs,
            device_id=dev, device_id_type=MESH,
        )
        c.start()
        sends.append(c)

    def landed(ref, sem):
        pltpu.make_async_copy(ref, ref, sem).wait()

    for d in zpeer:
        send(grad.at[:, lo], ga.at[yh, zl], garecv.at[yh, zl], d)
    for d in yfar:
        send(grad.at[:, hi], gb.at[yh, zl], gbrecv.at[yh, zl], d)
    send(ob, bbuf.at[par, 0], brecv.at[par, 0], mate[0])
    for d in yfar:
        send(grad.at[:, lo], ga.at[yh, zl], garecv.at[yh, zl], d)
    for d in zpeer:
        send(grad.at[:, hi], gb.at[yh, zl], gbrecv.at[yh, zl], d)
    for k, d in xpeer.items():
        send(ob, bbuf.at[par, NX - k], brecv.at[par, NX - k], d)

    local[0].wait()
    local[1].wait()
    mine = sbuf.at[par, yh, zl]
    for h in range(HEADS):
        cut = slice(h * HD, (h + 1) * HD)
        rot = jnp.dot(inp_v[:, cut], basis_v[h], preferred_element_type=F32)
        mine[:, cut] = (rot * rot).astype(BF16)

    def slot(y_, z_):
        return sbuf.at[y_ % NQ, y_ // NQ, z_], srecv.at[y_, z_]

    zs = [(zl + k) % NZ for k in (0, 1, 3, 2)]

    def hop(d, zz=None):
        up, down = (y + NY - d) % NY, (y + d) % NY
        for i, z_ in enumerate(zs):
            if zz is not None and not any(z_ is w for w in zz):
                continue
            if d or i:
                landed(*slot(up, z_))
            if d < 3 or i < 2:
                ref, sem = slot(up, z_)
                send(ref, ref, sem, yup)
            if d:
                landed(*slot(down, z_))
            if d < 3 or i >= 2:
                ref, sem = slot(down, z_)
                send(ref, ref, sem, ydown)

    for d in zpeer:
        ref, sem = slot(y, zl)
        send(ref, ref, sem, d)
    hop(0, zs[:1])

    for z_ in zs[1:]:
        landed(ga.at[yh, z_], garecv.at[yh, z_])
        for d in yfar:
            send(ga.at[yh, z_], ga.at[yh, z_], garecv.at[yh, z_], d)
    hs = [(yh + k) % NP for k in (0, 1, 3, 2)]
    for h_ in hs[1:]:
        landed(gb.at[h_, zl], gbrecv.at[h_, zl])
        for d in zpeer:
            send(gb.at[h_, zl], gb.at[h_, zl], gbrecv.at[h_, zl], d)
    other = 1 - par
    landed(bbuf.at[other, 0], brecv.at[other, 0])
    for k, d in xpeer.items():
        send(bbuf.at[other, 0], bbuf.at[other, NX - k], brecv.at[other, NX - k], d)

    hop(0, zs[1:])
    hop(1)
    local[2].wait()
    local[3].wait()
    local[4].wait()
    for h_ in hs[1:]:
        for z_ in zs:
            landed(ga.at[h_, z_], garecv.at[h_, z_])
    for z_ in zs[1:]:
        for h_ in hs:
            landed(gb.at[h_, z_], gbrecv.at[h_, z_])

    for q in (other, par):
        for k in (1, 3, 2):
            landed(bbuf.at[q, k], brecv.at[q, k])
        nt = (((1,), (1,)), ((), ()))
        lhs = bbuf[q].reshape(NX * COLS, FEAT)
        p = lax.dot_general(lhs[:, :FH], ga[...].reshape(PTOK, FH), nt, preferred_element_type=F32)
        p = p + lax.dot_general(lhs[:, FH:], gb[...].reshape(PTOK, FH), nt, preferred_element_type=F32)
        p = p.reshape(NH, NC, SLICE, PTOK)
        for c in range(NC):
            part[c, q] = p[:, c]
        send(part.at[1 - core, q], sib_in.at[q], crecv.at[q], twin)
    for q in (other, par):
        landed(sib_in.at[q], crecv.at[q])
        psum[q] = part[core, q] + sib_in[q]
        for i, d in enumerate(hpeer):
            send(psum.at[q, (zh + 1 + i) % NH], zin.at[q, 1 - i], zrecv.at[q, 1 - i], d)
    hop(2)
    for q in (other, par):
        acc = psum[q, zh]
        for i in range(NH - 1):
            landed(zin.at[q, i], zrecv.at[q, i])
            acc = acc + zin[q, i]
        val = (acc * acc).astype(BF16)
        if q is other:
            away[...] = val
            for d in mate:
                send(away, sq.at[par, tensor], qrecv.at[par, tensor], d)
        else:
            sq[par, tensor] = val
            for d in hpeer + [twin]:
                send(sq.at[par, tensor], sq.at[par, tensor], qrecv.at[par, tensor], d)
    hop(3)
    same = [((zh + a) % NH) * NC + core for a in range(NH)]
    across = [((zh + a) % NH) * NC + 1 - core for a in range(NH)]
    for q, js in ((other, same), (par, same[1:])):
        for j in js:
            landed(sq.at[q, j], qrecv.at[q, j])
            send(sq.at[q, j], sq.at[q, j], qrecv.at[q, j], twin)
    for z_ in zs:
        landed(*slot((y + 4) % NY, z_))
    for q in (other, par):
        for j in across:
            landed(sq.at[q, j], qrecv.at[q, j])

    for n in range(2):
        acc = None
        for q in range(NQ):
            rhs = sbuf[q, :, :, :, n * FH : (n + 1) * FH].reshape(PTOK, FH)
            p = jnp.dot(sq[q].reshape(NX * COLS, PTOK), rhs, preferred_element_type=F32)
            acc = p if acc is None else acc + p
        eig[n] = acc.reshape(NX, COLS, FH)
        for k, d in xpeer.items():
            send(eig.at[n, k], eig_in.at[n, NX - k - 1], erecv.at[n, NX - k - 1], d)
    for n in range(2):
        acc = eig[n, 0]
        for k in (0, 2, 1):
            landed(eig_in.at[n, k], erecv.at[n, k])
            acc = acc + eig_in[n, k]
        out[:, n * FH : (n + 1) * FH] = acc * F32(1.0 / TOKENS)
    for c in sends:
        c.wait_send()


def per_device(inputs, in_basis, out_grads, out_basis):
    dma = pltpu.SemaphoreType.DMA
    hbm = pl.BlockSpec(memory_space=pltpu.HBM)
    eigen = pl.pallas_call(
        kernel,
        out_shape=jax.ShapeDtypeStruct((COLS, FEAT), F32),
        in_specs=[hbm] * 4,
        out_specs=pl.BlockSpec(memory_space=pltpu.VMEM),
        scratch_shapes=[
            pltpu.VMEM((NP, NZ, TOK, FH), BF16),
            pltpu.VMEM((NP, NZ, TOK, FH), BF16),
            pltpu.VMEM((NQ, NP, NZ, TOK, FEAT), BF16),
            pltpu.VMEM((NQ, NX, COLS, FEAT), BF16),
            pltpu.VMEM((TOK, FEAT), BF16),
            pltpu.VMEM((HEADS, HD, HD), BF16),
            pltpu.VMEM((NC, NQ, NH, SLICE, PTOK), F32),
            pltpu.VMEM((NQ, NH, SLICE, PTOK), F32),
            pltpu.VMEM((NQ, NH, SLICE, PTOK), F32),
            pltpu.VMEM((NQ, NH - 1, SLICE, PTOK), F32),
            pltpu.VMEM((SLICE, PTOK), BF16),
            pltpu.VMEM((NQ, NT, SLICE, PTOK), BF16),
            pltpu.VMEM((2, NX, COLS, FH), F32),
            pltpu.VMEM((2, NX - 1, COLS, FH), F32),
            dma((5,)),
            dma((SENDS,)),
            dma((NP, NZ)),
            dma((NP, NZ)),
            dma((NY, NZ)),
            dma((NQ, NX)),
            dma((NQ,)),
            dma((NQ, NH - 1)),
            dma((NQ, NT)),
            dma((2, NX - 1)),
        ],
        compiler_params=pltpu.CompilerParams(
            collective_id=0, has_side_effects=True, vmem_limit_bytes=24 << 20
        ),
        cost_estimate=pl.CostEstimate(flops=4 * 10**8, bytes_accessed=10**6, transcendentals=0),
        name="eigen_fit",
    )(*(pltpu.with_memory_space_constraint(a, pltpu.HBM) for a in (inputs, in_basis, out_grads, out_basis.T)))
    return eigen.T


def solution(mesh):
    in_specs = (P("dp", "tensor"), P("tensor", None, None), P("dp", "tensor"), P("tensor", "dp"))
    out_specs = P("tensor", "dp")
    return jax.shard_map(
        per_device, mesh=mesh, in_specs=in_specs, out_specs=out_specs, check_vma=False
    )
```

```python
import jax
import jax.numpy as jnp
from jax import lax
from jax.experimental import pallas as pl
from jax.experimental.pallas import tpu as pltpu
from jax.sharding import PartitionSpec as P

MESH = pl.DeviceIdType.MESH
BF16, F32 = jnp.bfloat16, jnp.float32
NZ, NX, NY, NH, NC = 4, 4, 8, 3, 2
NT = NH * NC
NQ = 2
NP = NY // NQ
TOK, FEAT, COLS = 16, 1024, 48
FH = FEAT // 2
HEADS, HD = 8, 128
TOKENS = 2048
PTOK = NP * NZ * TOK
NA = 2
SLICE = NX * COLS // NT // NA
SENDS = 160
XSLOT = (1, 2, 0, 3)


def kernel(
    inp, basis, grad, ob, out,
    ga, gb, sbuf, bbuf, inp_v, basis_v, part, sib_in, psum, zin, away, sq, eig, eig_in, passing,
    lsem, ssem, garecv, gbrecv, srecv, brecv, crecv, zrecv, qrecv, erecv, precv,
):
    dp, tensor = lax.axis_index("dp"), lax.axis_index("tensor")
    zl, x, y = dp // (NX * NY), (dp // NY) % NX, dp % NY
    zh, core = tensor // NC, tensor % NC
    par, yh = y % NQ, y // NQ
    ymate = y + 1 - 2 * par

    def device(z_, x_, y_, h_=None):
        place = (z_ % NZ) * NX * NY + (x_ % NX) * NY + y_ % NY
        return (place, tensor if h_ is None else (h_ % NH) * NC + core)

    zpeer = [device(zl + k, x, y) for k in (2, 1, 3)]
    xpeer = {k: device(zl, x + k, y) for k in (2, 1, 3)}
    yfar = [device(zl, x, y + k) for k in (4, 2, 6)]
    yup, ydown = device(zl, x, y + 1), device(zl, x, y + NY - 1)
    mate = [device(zl, x, ymate, zh + a) for a in range(NH)]
    hpeer = [device(zl, x, y, zh + a) for a in (1, 2)]
    twin = (dp, zh * NC + 1 - core)

    peers = zpeer + list(xpeer.values()) + yfar + [yup, ydown] + mate[1:] + hpeer + [twin]
    barrier = pltpu.get_barrier_semaphore()
    for p in peers:
        pl.semaphore_signal(barrier, inc=1, device_id=p, device_id_type=MESH)

    lo, hi = pl.ds(0, FH), pl.ds(FH, FH)
    local = [
        pltpu.make_async_copy(inp, inp_v, lsem.at[0]),
        pltpu.make_async_copy(basis, basis_v, lsem.at[1]),
        pltpu.make_async_copy(grad.at[:, lo], ga.at[yh, zl], lsem.at[2]),
        pltpu.make_async_copy(grad.at[:, hi], gb.at[yh, zl], lsem.at[3]),
        pltpu.make_async_copy(ob, bbuf.at[par, XSLOT[0]], lsem.at[4]),
    ]
    for c in local:
        c.start()
    pl.semaphore_wait(barrier, len(peers))

    sends = []

    def send(src, dst, rs, dev):
        c = pltpu.make_async_remote_copy(
            src_ref=src, dst_ref=dst, send_sem=ssem.at[len(sends)], recv_sem=rs,
            device_id=dev, device_id_type=MESH,
        )
        c.start()
        sends.append(c)

    def landed(ref, sem):
        pltpu.make_async_copy(ref, ref, sem).wait()

    for d in zpeer:
        send(grad.at[:, lo], ga.at[yh, zl], garecv.at[yh, zl], d)
    for d in yfar:
        send(grad.at[:, hi], gb.at[yh, zl], gbrecv.at[yh, zl], d)
    send(ob, bbuf.at[par, XSLOT[0]], brecv.at[par, 0], mate[0])
    for d in yfar:
        send(grad.at[:, lo], ga.at[yh, zl], garecv.at[yh, zl], d)
    for d in zpeer:
        send(grad.at[:, hi], gb.at[yh, zl], gbrecv.at[yh, zl], d)
    for k, d in xpeer.items():
        send(ob, bbuf.at[par, XSLOT[NX - k]], brecv.at[par, NX - k], d)

    local[0].wait()
    local[1].wait()
    mine = sbuf.at[par, yh, zl]
    for h in range(HEADS):
        cut = slice(h * HD, (h + 1) * HD)
        rot = jnp.dot(inp_v[:, cut], basis_v[h], preferred_element_type=F32)
        mine[:, cut] = (rot * rot).astype(BF16)

    def slot(y_, z_):
        return sbuf.at[y_ % NQ, y_ // NQ, z_], srecv.at[y_, z_]

    zs = [(zl + k) % NZ for k in (0, 1, 3, 2)]

    def hop(d, zz=None):
        up, down = (y + NY - d) % NY, (y + d) % NY
        for i, z_ in enumerate(zs):
            if zz is not None and not any(z_ is w for w in zz):
                continue
            if d or i:
                landed(*slot(up, z_))
            if d < 3 or i < 2:
                ref, sem = slot(up, z_)
                send(ref, ref, sem, yup)
            if d:
                landed(*slot(down, z_))
            if d < 3 or i >= 2:
                ref, sem = slot(down, z_)
                send(ref, ref, sem, ydown)

    for d in zpeer:
        ref, sem = slot(y, zl)
        send(ref, ref, sem, d)
    hop(0, zs[:1])

    for z_ in zs[1:]:
        landed(ga.at[yh, z_], garecv.at[yh, z_])
        for d in yfar:
            send(ga.at[yh, z_], ga.at[yh, z_], garecv.at[yh, z_], d)
    other = 1 - par
    landed(bbuf.at[other, XSLOT[0]], brecv.at[other, 0])
    for k, d in xpeer.items():
        send(bbuf.at[other, XSLOT[0]], bbuf.at[other, XSLOT[NX - k]], brecv.at[other, NX - k], d)

    hs = [(yh + k) % NP for k in (0, 1, 3, 2)]
    for h_ in hs[1:]:
        landed(gb.at[h_, zl], gbrecv.at[h_, zl])
        for d in zpeer:
            send(gb.at[h_, zl], gb.at[h_, zl], gbrecv.at[h_, zl], d)
    hop(0, zs[1:])
    hop(1)
    local[2].wait()
    local[3].wait()
    local[4].wait()
    for h_ in hs[1:]:
        for z_ in zs:
            landed(ga.at[h_, z_], garecv.at[h_, z_])
    for z_ in zs[1:]:
        for h_ in hs:
            landed(gb.at[h_, z_], gbrecv.at[h_, z_])

    for q in (other, par):
        for k in (2, 1, 3):
            landed(bbuf.at[q, XSLOT[k]], brecv.at[q, k])
    nt = (((1,), (1,)), ((), ()))
    groups = [(a, q) for a in range(NA) for q in (other, par)]
    for a, q in groups:
        lhs = bbuf[q, 2 * a : 2 * a + 2].reshape(2 * COLS, FEAT)
        p = lax.dot_general(lhs[:, :FH], ga[...].reshape(PTOK, FH), nt, preferred_element_type=F32)
        p = p + lax.dot_general(lhs[:, FH:], gb[...].reshape(PTOK, FH), nt, preferred_element_type=F32)
        p = p.reshape(NH, NC, SLICE, PTOK)
        for c in range(NC):
            part[c, a, q] = p[:, c]
        send(part.at[1 - core, a, q], sib_in.at[a, q], crecv.at[a, q], twin)
    for a, q in groups:
        landed(sib_in.at[a, q], crecv.at[a, q])
        psum[a, q] = part[core, a, q] + sib_in[a, q]
        for i, d in enumerate(hpeer):
            send(psum.at[a, q, (zh + 1 + i) % NH], zin.at[a, q, 1 - i], zrecv.at[a, q, 1 - i], d)
    hop(2)
    for a, q in groups:
        acc = psum[a, q, zh]
        for i in range(NH - 1):
            landed(zin.at[a, q, i], zrecv.at[a, q, i])
            acc = acc + zin[a, q, i]
        val = (acc * acc).astype(BF16)
        if q is other:
            away[a] = val
            for d in mate:
                send(away.at[a], sq.at[a, par, tensor], qrecv.at[a, par, tensor], d)
        else:
            sq[a, par, tensor] = val
            for d in hpeer + [twin]:
                send(sq.at[a, par, tensor], sq.at[a, par, tensor], qrecv.at[a, par, tensor], d)
    hop(3)
    same = [((zh + b) % NH) * NC + core for b in range(NH)]
    across = [((zh + b) % NH) * NC + 1 - core for b in range(NH)]

    for a in range(NA):
        for q, js in ((other, same), (par, same[1:])):
            for j in js:
                landed(sq.at[a, q, j], qrecv.at[a, q, j])
                send(sq.at[a, q, j], sq.at[a, q, j], qrecv.at[a, q, j], twin)
        if a == 0:
            for z_ in zs:
                landed(*slot((y + 4) % NY, z_))
        for q in (other, par):
            for j in across:
                landed(sq.at[a, q, j], qrecv.at[a, q, j])
        for n in range(2):
            acc = None
            for q in range(NQ):
                rhs = sbuf[q, :, :, :, n * FH : (n + 1) * FH].reshape(PTOK, FH)
                p = jnp.dot(sq[a, q].reshape(2 * COLS, PTOK), rhs, preferred_element_type=F32)
                acc = p if acc is None else acc + p
            eig[n, 2 * a : 2 * a + 2] = acc.reshape(2, COLS, FH)
            if a == 0:
                to = xpeer[1] if n == 0 else xpeer[3]
                send(eig.at[n, XSLOT[2]], passing.at[n], precv.at[n], to)
        if a == 1:
            send(eig.at[1, XSLOT[1]], eig_in.at[1, 0], erecv.at[1, 0], xpeer[1])
            send(eig.at[0, XSLOT[3]], eig_in.at[0, 0], erecv.at[0, 0], xpeer[3])
    for n, k in ((0, 1), (1, 3)):
        landed(passing.at[n], precv.at[n])
        eig[n, XSLOT[k]] = eig[n, XSLOT[k]] + passing[n]
        send(eig.at[n, XSLOT[k]], eig_in.at[n, 1], erecv.at[n, 1], xpeer[k])
    for n in range(2):
        acc = eig[n, XSLOT[0]]
        for k in range(2):
            landed(eig_in.at[n, k], erecv.at[n, k])
            acc = acc + eig_in[n, k]
        out[:, n * FH : (n + 1) * FH] = acc * F32(1.0 / TOKENS)
    for c in sends:
        c.wait_send()


def per_device(inputs, in_basis, out_grads, out_basis):
    dma = pltpu.SemaphoreType.DMA
    hbm = pl.BlockSpec(memory_space=pltpu.HBM)
    eigen = pl.pallas_call(
        kernel,
        out_shape=jax.ShapeDtypeStruct((COLS, FEAT), F32),
        in_specs=[hbm] * 4,
        out_specs=pl.BlockSpec(memory_space=pltpu.VMEM),
        scratch_shapes=[
            pltpu.VMEM((NP, NZ, TOK, FH), BF16),
            pltpu.VMEM((NP, NZ, TOK, FH), BF16),
            pltpu.VMEM((NQ, NP, NZ, TOK, FEAT), BF16),
            pltpu.VMEM((NQ, NX, COLS, FEAT), BF16),
            pltpu.VMEM((TOK, FEAT), BF16),
            pltpu.VMEM((HEADS, HD, HD), BF16),
            pltpu.VMEM((NC, NA, NQ, NH, SLICE, PTOK), F32),
            pltpu.VMEM((NA, NQ, NH, SLICE, PTOK), F32),
            pltpu.VMEM((NA, NQ, NH, SLICE, PTOK), F32),
            pltpu.VMEM((NA, NQ, NH - 1, SLICE, PTOK), F32),
            pltpu.VMEM((NA, SLICE, PTOK), BF16),
            pltpu.VMEM((NA, NQ, NT, SLICE, PTOK), BF16),
            pltpu.VMEM((2, NX, COLS, FH), F32),
            pltpu.VMEM((2, 2, COLS, FH), F32),
            pltpu.VMEM((2, COLS, FH), F32),
            dma((5,)),
            dma((SENDS,)),
            dma((NP, NZ)),
            dma((NP, NZ)),
            dma((NY, NZ)),
            dma((NQ, NX)),
            dma((NA, NQ)),
            dma((NA, NQ, NH - 1)),
            dma((NA, NQ, NT)),
            dma((2, 2)),
            dma((2,)),
        ],
        compiler_params=pltpu.CompilerParams(
            collective_id=0, has_side_effects=True, vmem_limit_bytes=24 << 20
        ),
        cost_estimate=pl.CostEstimate(flops=4 * 10**8, bytes_accessed=10**6, transcendentals=0),
        name="eigen_fit",
    )(*(pltpu.with_memory_space_constraint(a, pltpu.HBM) for a in (inputs, in_basis, out_grads, out_basis.T)))
    return eigen.T


def solution(mesh):
    in_specs = (P("dp", "tensor"), P("tensor", None, None), P("dp", "tensor"), P("tensor", "dp"))
    out_specs = P("tensor", "dp")
    return jax.shard_map(
        per_device, mesh=mesh, in_specs=in_specs, out_specs=out_specs, check_vma=False
    )
```
